512 devices in a mesh: rep: 64 (over y, z_hi, x, core), fsdp: 8 (over z_lo).
Axes of the slice: x: 4, y: 4, z: 16 (z_hi: 2, z_lo: 8; z = z_hi * 8 + z_lo), core: 2. Of those that a mesh axis runs over, the one named last changes fastest.
Arguments:
- local_weights: bfloat16 [64, 64, 6144], P('rep', 'fsdp'), may hold values from -16 to 16
- base_weights: float32 [64, 6144], P('fsdp'), may hold values from -6 to 6
- momentum: float32 [64, 6144], P('fsdp'), may hold values from -4 to 4
- scale_codes: int32 [64, 64, 48], P('rep', 'fsdp'), may hold values from 16 to 64
Outputs:
- new_base: float32 [64, 6144], P('fsdp')
- new_momentum: float32 [64, 6144], P('fsdp')
- full_fragment: bfloat16 [64, 6144], replicated
The draws below stay inside these ranges and needn't reach their ends.
All inputs are finite; a program needn't handle non-finite values.
Results may differ from the reference program's by a relative error of at most 0.009.
Values may be sent and summed in bfloat16 or wider, within the bound.
A program may use at most 64 MiB of HBM per device.

```python
import jax
import jax.numpy as jnp

D = 6144
QBLK = 128
NCOL = 48
ROWS = 64
N_REP = 64


def plant(array, key, least, high):
    shape = array.shape
    place = [jax.random.randint(jax.random.fold_in(key, axis), (), 0, shape[axis]) for axis in range(len(shape))]
    array = array.at[tuple(place)].set(least)
    longest = shape.index(max(shape))
    place[longest] = (place[longest] + 1) % shape[longest]
    return array.at[tuple(place)].set(high)


def raised(entries, rng, source, target, parts, factor):
    def block_of(axis_at):
        return (jnp.arange(entries.shape[axis_at]) // (entries.shape[axis_at] // parts)).reshape((-1,) + (1,) * (entries.ndim - 1 - axis_at))

    one_side = jax.random.permutation(rng, parts)[block_of(target)]
    far = (block_of(target) + parts // 2) % parts
    return jnp.where((block_of(source) == one_side) | (block_of(source) == far), factor * entries, entries)


def levels(own_key, shape, shards, low, high):
    gain, own = 1.0, jax.random.fold_in(own_key, 6)
    for dim, blocks in shards:
        draws = jnp.exp(jax.random.uniform(jax.random.fold_in(own, dim), (blocks,), jnp.float32, low / len(shards), high / len(shards)))
        gain = gain * jnp.repeat(draws, shape[dim] // blocks).reshape([-1 if axis == dim else 1 for axis in range(len(shape))])
    return gain


def scatter_about(key, extent, width, bound, cuts=(), kind=jnp.bfloat16):
    gain = levels(key, extent, cuts, -0.22, 0.18) if cuts else 1.0
    result = jax.random.normal(key, extent, jnp.float32) * width * gain
    return jnp.minimum(jnp.maximum(result, -bound), bound).astype(kind)


def bell_draw_with(stream_key, extent, spread, reach, shards, heavy, dtype=jnp.bfloat16):
    entries = spread * jax.random.normal(stream_key, extent, jnp.float32)
    if shards:
        entries = entries * levels(stream_key, extent, shards, -0.22, 0.18)
    return jnp.clip(raised(entries, jax.random.fold_in(stream_key, 3), *heavy), -reach, reach).astype(dtype)


def setup_inputs(seed: int = 0) -> dict:
    streams_of = jax.random.split(jax.random.key(seed), 5)
    return {
        "local_weights": bell_draw_with(streams_of[0], (N_REP, ROWS, D), 1.0, 16.0, ((0, 64), (1, 8)), (0, 2, 64, 4.0)),
        "base_weights": scatter_about(streams_of[1], (ROWS, D), 1.0, 6.0, ((0, 8),), jnp.float32),
        "momentum": scatter_about(streams_of[2], (ROWS, D), 0.5, 4.0, ((0, 8),), jnp.float32),
        "scale_codes": plant(jax.random.randint(streams_of[3], (N_REP, ROWS, NCOL), 16, 65), jax.random.fold_in(streams_of[3], 1), 16, 64).astype(jnp.int32),
    }


outer_rate = 0.7
outer_mu = 0.9
clip_level = 4.0


def reference(local_weights, base_weights, momentum, scale_codes):
    scales = jnp.repeat(scale_codes.astype(jnp.float32) / 64.0, QBLK, axis=2)
    pseudo = base_weights[None] - local_weights.astype(jnp.float32)
    quantized = jnp.clip(pseudo / scales, -clip_level, clip_level).astype(jnp.bfloat16)
    summed = jnp.sum(quantized.astype(jnp.float32) * scales, axis=0)
    average = summed / N_REP
    new_momentum = outer_mu * momentum + average
    new_base = base_weights - outer_rate * (average + outer_mu * new_momentum)
    return new_base, new_momentum, new_base.astype(jnp.bfloat16)
```

```python
import jax
import jax.numpy as jnp
from jax import lax
from jax.experimental import pallas as pl
from jax.experimental.pallas import tpu as pltpu
from jax.sharding import PartitionSpec as P

outer_rate = 0.7
outer_mu = 0.9
clip_level = 4.0

ROWS = 8
COLS = 6144
LANES = 128
UNIT = 256
UNITS = COLS // UNIT
PLANE = 32
Z = 16
FSDP = 8
REPLICAS = 64
MESH = pl.DeviceIdType.MESH

OFFSETS = sorted(
    [(dx, dy) for dy in range(4) for dx in range(4)],
    key=lambda o: -(min(o[0], 4 - o[0]) + min(o[1], 4 - o[1])),
)


def kernel(local_hbm, base_hbm, moment_hbm, codes_hbm, new_base_ref, new_moment_ref, full_ref,
           local, base, moment, codes, terms, arrived, partials, us, rows,
           load_sem, term_send, term_recv, u_send, u_recv, part_send, part_recv, row_send, sib_send, row_recv, out_sem):
    rep = lax.axis_index("rep")
    zl = lax.axis_index("fsdp")
    c = rep % 2
    x = (rep // 2) % 4
    zh = (rep // 8) % 2
    y = rep // 16
    z = zh * FSDP + zl
    even = (x + y) % 2 == 0
    owner = jnp.logical_or(c == 0, even)
    my_unit = jnp.where(c == 0, y * 4 + x, 16 + y * 2 + x // 2)
    xs = [(x + d) % 4 for d in range(4)]
    ys = [(y + d) % 4 for d in range(4)]

    def in_plane(px, py, pc):
        return (py * 16 + zh * 8 + px * 2 + pc, zl)

    def along_z(d):
        zt = (z + d + Z) % Z
        return (y * 16 + (zt // FSDP) * 8 + x * 2 + c, zt % FSDP)

    loads = [
        pltpu.make_async_copy(src, dst, load_sem.at[i])
        for i, (src, dst) in enumerate(((codes_hbm, codes), (local_hbm, local), (base_hbm, base), (moment_hbm, moment)))
    ]
    for load in loads:
        load.start()

    barrier = pltpu.get_barrier_semaphore()
    z_near = (4, -4, 3, -3, 2, -2, 1, -1)
    for d in z_near:
        pl.semaphore_signal(barrier, inc=1, device_id=along_z(d), device_id_type=MESH)
    for dx, dy in OFFSETS:
        for pc in (c, 1 - c) if (dx, dy) != (0, 0) else (1 - c,):
            pl.semaphore_signal(barrier, inc=1, device_id=in_plane(xs[dx], ys[dy], pc), device_id_type=MESH)

    for load in loads:
        load.wait()

    scales = codes[0].astype(jnp.float32) / 64.0
    inverse = 1.0 / scales

    def term(j):
        cols = slice(j * LANES, (j + 1) * LANES)
        pseudo = base[:, cols] - local[0, :, cols].astype(jnp.float32)
        quantized = jnp.clip(pseudo * inverse[:, j:j + 1], -clip_level, clip_level).astype(jnp.bfloat16)
        return quantized.astype(jnp.float32) * scales[:, j:j + 1]

    for unit in range(UNITS):
        terms[unit] = jnp.concatenate([term(2 * unit), term(2 * unit + 1)], axis=0).astype(jnp.bfloat16)

    halves = []
    for half in range(2):
        cols = pl.ds(pl.multiple_of(my_unit * UNIT + half * LANES, LANES), LANES)
        halves.append(base[:, cols] - (outer_rate * outer_mu * outer_mu) * moment[:, cols])

    @pl.when(owner)
    def _():
        us[zl] = jnp.concatenate(halves, axis=0)

    pl.semaphore_wait(barrier, len(z_near) + PLANE - 1)

    def send_term(px, py, pc, to_core):
        unit = py * 4 + px if to_core == 0 else 16 + py * 2 + px // 2
        slot = (((py - y + 4) % 4) * 4 + (px - x + 4) % 4) * 2 + (c if to_core == 0 else 1 - c) - 1
        pltpu.make_async_remote_copy(
            src_ref=terms.at[unit], dst_ref=arrived.at[slot], send_sem=term_send, recv_sem=term_recv,
            device_id=in_plane(px, py, pc), device_id_type=MESH,
        ).start()

    second = [(dx2, dy) for dy in (2, 1, 3, 0) for dx2 in (1, 0)]
    for i, (dx, dy) in enumerate(OFFSETS):
        if (dx, dy) == (0, 0):
            @pl.when(c == 1)
            def _():
                send_term(x, y, 0, 0)
        else:
            send_term(xs[dx], ys[dy], 0, 0)
        if i % 2 == 1:
            dx2, sy = second[i // 2]
            px = ys[sy] % 2 + 2 * ((x // 2 + dx2) % 2)
            if (dx2, sy) == (0, 0):
                @pl.when(jnp.logical_not(jnp.logical_and(c == 1, even)))
                def _():
                    send_term(px, ys[sy], 1, 1)
            else:
                send_term(px, ys[sy], 1, 1)

    def send(src, dst, send_sem, recv_sem, to):
        return pltpu.make_async_remote_copy(
            src_ref=src, dst_ref=dst, send_sem=send_sem, recv_sem=recv_sem, device_id=to, device_id_type=MESH)

    @pl.when(owner)
    def _():
        for d in (4, 3, -3, 2, -2, 1, -1):
            send(us.at[zl], us.at[zl], u_send, u_recv, along_z(d)).start()

        pltpu.make_async_copy(arrived, arrived, term_recv).wait()
        total = terms[my_unit].astype(jnp.float32)
        for slot in range(PLANE - 1):
            total += arrived[slot].astype(jnp.float32)
        partials[z] = total.astype(jnp.bfloat16)
        pltpu.make_async_copy(us.at[0:FSDP - 1], us.at[0:FSDP - 1], u_recv).wait()

        for d in (8, 7, -7, 6, -6, 5, -5, 4, -4, 3, -3, 2, -2, 1, -1):
            send(partials.at[z], partials.at[z], part_send, part_recv, along_z(d)).start()
        pltpu.make_async_copy(partials.at[0:Z - 1], partials.at[0:Z - 1], part_recv).wait()

        def summed(f):
            return partials[f].astype(jnp.float32) + partials[f + FSDP].astype(jnp.float32)

        updated = [us[f] - (outer_rate * (1.0 + outer_mu) / REPLICAS) * summed(f) for f in range(FSDP)]
        mine = summed(zl)
        high = mine.astype(jnp.bfloat16).astype(jnp.float32)
        low = mine - high
        for half in range(2):
            cols = pl.ds(pl.multiple_of(my_unit * UNIT + half * LANES, LANES), LANES)
            part = slice(half * ROWS, (half + 1) * ROWS)
            for g in range(FSDP // 2):
                pair = jnp.concatenate([updated[2 * g][part], updated[2 * g + 1][part]], axis=0)
                rows[16 * g:16 * g + 16, cols] = pair.astype(jnp.bfloat16)
            rows[64:80, cols] = jnp.concatenate([high[part], low[part]], axis=0).astype(jnp.bfloat16)

        block = rows.at[:, pl.ds(pl.multiple_of(my_unit * UNIT, UNIT), UNIT)]
        for dx, dy in OFFSETS:
            if (dx, dy) != (0, 0):
                send(block, block, row_send, row_recv, in_plane(xs[dx], ys[dy], c)).start()
            send(block, block, sib_send, row_recv, in_plane(xs[dx], ys[dy], 1 - c)).start()
        others = rows.at[:, 0:(UNITS - 1) * UNIT]
        pltpu.make_async_copy(others, others, row_recv).wait()

    @pl.when(jnp.logical_not(owner))
    def _():
        pltpu.make_async_copy(rows, rows, row_recv).wait()

    full_copy = pltpu.make_async_copy(rows.at[0:64], full_ref, out_sem)
    full_copy.start()
    for j in range(COLS // LANES):
        cols = slice(j * LANES, (j + 1) * LANES)
        split = rows[64:80, cols].astype(jnp.float32)
        average = (split[0:ROWS] + split[ROWS:2 * ROWS]) / REPLICAS
        new_moment = outer_mu * moment[:, cols] + average
        new_moment_ref[:, cols] = new_moment
        new_base_ref[:, cols] = base[:, cols] - outer_rate * (average + outer_mu * new_moment)
    full_copy.wait()

    @pl.when(owner)
    def _():
        own = terms.at[0:UNITS - 1]
        pltpu.make_async_copy(own, own, term_send).wait()
        pltpu.make_async_copy(us.at[0:FSDP - 1], us.at[0:FSDP - 1], u_send).wait()
        pltpu.make_async_copy(partials.at[0:Z - 1], partials.at[0:Z - 1], part_send).wait()
        sent = rows.at[:, 0:15 * UNIT]
        pltpu.make_async_copy(sent, sent, row_send).wait()
        sent = rows.at[:, 0:16 * UNIT]
        pltpu.make_async_copy(sent, sent, sib_send).wait()

    @pl.when(jnp.logical_not(owner))
    def _():
        pltpu.make_async_copy(terms, terms, term_send).wait()


def step(local_weights, base_weights, momentum, scale_codes):
    anywhere = pl.BlockSpec(memory_space=pl.ANY)
    vmem = pl.BlockSpec(memory_space=pltpu.VMEM)
    dma = pltpu.SemaphoreType.DMA
    return pl.pallas_call(
        kernel,
        out_shape=(
            jax.ShapeDtypeStruct((ROWS, COLS), jnp.float32),
            jax.ShapeDtypeStruct((ROWS, COLS), jnp.float32),
            jax.ShapeDtypeStruct((FSDP * ROWS, COLS), jnp.bfloat16),
        ),
        in_specs=[anywhere] * 4,
        out_specs=(vmem, vmem, anywhere),
        scratch_shapes=[
            pltpu.VMEM((1, ROWS, COLS), jnp.bfloat16),
            pltpu.VMEM((ROWS, COLS), jnp.float32),
            pltpu.VMEM((ROWS, COLS), jnp.float32),
            pltpu.VMEM((1, ROWS, COLS // LANES), jnp.int32),
            pltpu.VMEM((UNITS, 16, LANES), jnp.bfloat16),
            pltpu.VMEM((PLANE - 1, 16, LANES), jnp.bfloat16),
            pltpu.VMEM((Z, 16, LANES), jnp.bfloat16),
            pltpu.VMEM((FSDP, 16, LANES), jnp.float32),
            pltpu.VMEM((80, COLS), jnp.bfloat16),
            dma((4,)), dma, dma, dma, dma, dma, dma, dma, dma, dma, dma,
        ],
        compiler_params=pltpu.CompilerParams(collective_id=0, has_side_effects=True, vmem_limit_bytes=16 * 1024 * 1024),
        name="outer_step",
    )(local_weights, base_weights, momentum, scale_codes)


def solution(mesh):
    in_specs = (P("rep", "fsdp", None), P("fsdp", None), P("fsdp", None), P("rep", "fsdp", None))
    out_specs = (P("fsdp", None), P("fsdp", None), P())
    return jax.shard_map(step, mesh=mesh, in_specs=in_specs, out_specs=out_specs, check_vma=False)
```

```python
import jax
import jax.numpy as jnp
from jax import lax
from jax.experimental import pallas as pl
from jax.experimental.pallas import tpu as pltpu
from jax.sharding import PartitionSpec as P

outer_rate = 0.7
outer_mu = 0.9
clip_level = 4.0

ROWS = 8
COLS = 6144
LANES = 128
UNIT = 256
UNITS = COLS // UNIT
PLANE = 32
Z = 16
FSDP = 8
REPLICAS = 64
MESH = pl.DeviceIdType.MESH

OFFSETS = sorted(
    [(dx, dy) for dy in range(4) for dx in range(4)],
    key=lambda o: -(min(o[0], 4 - o[0]) + min(o[1], 4 - o[1])),
)


def kernel(local_hbm, base_hbm, moment_hbm, codes_hbm, new_base_ref, new_moment_ref, rows,
           local, base, moment, codes, terms, arrived, partials, us,
           load_sem, term_send, term_recv, u_send, u_recv, part_send, part_recv, row_send, sib_send, row_recv):
    rep = lax.axis_index("rep")
    zl = lax.axis_index("fsdp")
    c = rep % 2
    x = (rep // 2) % 4
    zh = (rep // 8) % 2
    y = rep // 16
    z = zh * FSDP + zl
    even = (x + y) % 2 == 0
    owner = jnp.logical_or(c == 0, even)
    my_unit = jnp.where(c == 0, y * 4 + x, 16 + y * 2 + x // 2)
    xs = [(x + d) % 4 for d in range(4)]
    ys = [(y + d) % 4 for d in range(4)]

    def in_plane(px, py, pc):
        return (py * 16 + zh * 8 + px * 2 + pc, zl)

    def along_z(d):
        zt = (z + d + Z) % Z
        return (y * 16 + (zt // FSDP) * 8 + x * 2 + c, zt % FSDP)

    loads = [
        pltpu.make_async_copy(src, dst, load_sem.at[i])
        for i, (src, dst) in enumerate(((codes_hbm, codes), (local_hbm, local), (base_hbm, base), (moment_hbm, moment)))
    ]
    for load in loads:
        load.start()

    barrier = pltpu.get_barrier_semaphore()
    z_near = (4, -4, 3, -3, 2, -2, 1, -1)
    for d in z_near:
        pl.semaphore_signal(barrier, inc=1, device_id=along_z(d), device_id_type=MESH)
    for dx, dy in OFFSETS:
        for pc in (c, 1 - c) if (dx, dy) != (0, 0) else (1 - c,):
            pl.semaphore_signal(barrier, inc=1, device_id=in_plane(xs[dx], ys[dy], pc), device_id_type=MESH)

    for load in loads:
        load.wait()

    scales = codes[0].astype(jnp.float32) / 64.0
    inverse = 1.0 / scales

    def term(j):
        cols = slice(j * LANES, (j + 1) * LANES)
        pseudo = base[:, cols] - local[0, :, cols].astype(jnp.float32)
        quantized = jnp.clip(pseudo * inverse[:, j:j + 1], -clip_level, clip_level).astype(jnp.bfloat16)
        return quantized.astype(jnp.float32) * scales[:, j:j + 1]

    for unit in range(UNITS):
        terms[unit] = jnp.concatenate([term(2 * unit), term(2 * unit + 1)], axis=0).astype(jnp.bfloat16)

    halves = []
    for half in range(2):
        cols = pl.ds(pl.multiple_of(my_unit * UNIT + half * LANES, LANES), LANES)
        halves.append(base[:, cols] - (outer_rate * outer_mu * outer_mu) * moment[:, cols])

    @pl.when(owner)
    def _():
        us[zl] = jnp.concatenate(halves, axis=0)

    pl.semaphore_wait(barrier, len(z_near) + PLANE - 1)

    def send_term(px, py, pc, to_core):
        unit = py * 4 + px if to_core == 0 else 16 + py * 2 + px // 2
        slot = (((py - y + 4) % 4) * 4 + (px - x + 4) % 4) * 2 + (c if to_core == 0 else 1 - c) - 1
        pltpu.make_async_remote_copy(
            src_ref=terms.at[unit], dst_ref=arrived.at[slot], send_sem=term_send, recv_sem=term_recv,
            device_id=in_plane(px, py, pc), device_id_type=MESH,
        ).start()

    second = [(dx2, dy) for dy in (2, 1, 3, 0) for dx2 in (1, 0)]
    for i, (dx, dy) in enumerate(OFFSETS):
        if (dx, dy) == (0, 0):
            @pl.when(c == 1)
            def _():
                send_term(x, y, 0, 0)
        else:
            send_term(xs[dx], ys[dy], 0, 0)
        if i % 2 == 1:
            dx2, sy = second[i // 2]
            px = ys[sy] % 2 + 2 * ((x // 2 + dx2) % 2)
            if (dx2, sy) == (0, 0):
                @pl.when(jnp.logical_not(jnp.logical_and(c == 1, even)))
                def _():
                    send_term(px, ys[sy], 1, 1)
            else:
                send_term(px, ys[sy], 1, 1)

    def send(src, dst, send_sem, recv_sem, to):
        return pltpu.make_async_remote_copy(
            src_ref=src, dst_ref=dst, send_sem=send_sem, recv_sem=recv_sem, device_id=to, device_id_type=MESH)

    @pl.when(owner)
    def _():
        for d in (4, 3, -3, 2, -2, 1, -1):
            send(us.at[zl], us.at[zl], u_send, u_recv, along_z(d)).start()

        pltpu.make_async_copy(arrived, arrived, term_recv).wait()
        total = terms[my_unit].astype(jnp.float32)
        for slot in range(PLANE - 1):
            total += arrived[slot].astype(jnp.float32)
        partials[z] = total.astype(jnp.bfloat16)
        pltpu.make_async_copy(us.at[0:FSDP - 1], us.at[0:FSDP - 1], u_recv).wait()

        for d in (8, 7, -7, 6, -6, 5, -5, 4, -4, 3, -3, 2, -2, 1, -1):
            send(partials.at[z], partials.at[z], part_send, part_recv, along_z(d)).start()
        pltpu.make_async_copy(partials.at[0:Z - 1], partials.at[0:Z - 1], part_recv).wait()

        def summed(f):
            return partials[f].astype(jnp.float32) + partials[f + FSDP].astype(jnp.float32)

        updated = [us[f] - (outer_rate * (1.0 + outer_mu) / REPLICAS) * summed(f) for f in range(FSDP)]
        mine = summed(zl)
        high = mine.astype(jnp.bfloat16).astype(jnp.float32)
        low = mine - high
        for half in range(2):
            cols = pl.ds(pl.multiple_of(my_unit * UNIT + half * LANES, LANES), LANES)
            part = slice(half * ROWS, (half + 1) * ROWS)
            for g in range(FSDP // 2):
                pair = jnp.concatenate([updated[2 * g][part], updated[2 * g + 1][part]], axis=0)
                rows[16 * g:16 * g + 16, cols] = pair.astype(jnp.bfloat16)
            rows[64:80, cols] = jnp.concatenate([high[part], low[part]], axis=0).astype(jnp.bfloat16)

        block = rows.at[:, pl.ds(pl.multiple_of(my_unit * UNIT, UNIT), UNIT)]
        for dx, dy in OFFSETS:
            if (dx, dy) != (0, 0):
                send(block, block, row_send, row_recv, in_plane(xs[dx], ys[dy], c)).start()
            send(block, block, sib_send, row_recv, in_plane(xs[dx], ys[dy], 1 - c)).start()
        others = rows.at[:, 0:(UNITS - 1) * UNIT]
        pltpu.make_async_copy(others, others, row_recv).wait()

    @pl.when(jnp.logical_not(owner))
    def _():
        pltpu.make_async_copy(rows, rows, row_recv).wait()

    for j in range(COLS // LANES):
        cols = slice(j * LANES, (j + 1) * LANES)
        split = rows[64:80, cols].astype(jnp.float32)
        average = (split[0:ROWS] + split[ROWS:2 * ROWS]) / REPLICAS
        new_moment = outer_mu * moment[:, cols] + average
        new_moment_ref[:, cols] = new_moment
        new_base_ref[:, cols] = base[:, cols] - outer_rate * (average + outer_mu * new_moment)

    @pl.when(owner)
    def _():
        own = terms.at[0:UNITS - 1]
        pltpu.make_async_copy(own, own, term_send).wait()
        pltpu.make_async_copy(us.at[0:FSDP - 1], us.at[0:FSDP - 1], u_send).wait()
        pltpu.make_async_copy(partials.at[0:Z - 1], partials.at[0:Z - 1], part_send).wait()
        sent = rows.at[:, 0:15 * UNIT]
        pltpu.make_async_copy(sent, sent, row_send).wait()
        sent = rows.at[:, 0:16 * UNIT]
        pltpu.make_async_copy(sent, sent, sib_send).wait()

    @pl.when(jnp.logical_not(owner))
    def _():
        pltpu.make_async_copy(terms, terms, term_send).wait()


def finish(new_base, new_moment, rows, new_base_out, new_moment_out, full_out, sems):
    copies = [
        pltpu.make_async_copy(src, dst, sems.at[i])
        for i, (src, dst) in enumerate(((rows.at[0:64], full_out), (new_base, new_base_out), (new_moment, new_moment_out)))
    ]
    for copy in copies:
        copy.start()
    for copy in copies:
        copy.wait()


def step(local_weights, base_weights, momentum, scale_codes):
    anywhere = pl.BlockSpec(memory_space=pl.ANY)
    vmem = pl.BlockSpec(memory_space=pltpu.VMEM)
    dma = pltpu.SemaphoreType.DMA
    results = pl.pallas_call(
        kernel,
        out_shape=(
            pltpu.VMEM((ROWS, COLS), jnp.float32),
            pltpu.VMEM((ROWS, COLS), jnp.float32),
            pltpu.VMEM((80, COLS), jnp.bfloat16),
        ),
        in_specs=[pl.BlockSpec(memory_space=pltpu.HBM)] * 4,
        out_specs=(vmem, vmem, vmem),
        scratch_shapes=[
            pltpu.VMEM((1, ROWS, COLS), jnp.bfloat16),
            pltpu.VMEM((ROWS, COLS), jnp.float32),
            pltpu.VMEM((ROWS, COLS), jnp.float32),
            pltpu.VMEM((1, ROWS, COLS // LANES), jnp.int32),
            pltpu.VMEM((UNITS, 16, LANES), jnp.bfloat16),
            pltpu.VMEM((PLANE - 1, 16, LANES), jnp.bfloat16),
            pltpu.VMEM((Z, 16, LANES), jnp.bfloat16),
            pltpu.VMEM((FSDP, 16, LANES), jnp.float32),
            dma((4,)), dma, dma, dma, dma, dma, dma, dma, dma, dma,
        ],
        compiler_params=pltpu.CompilerParams(collective_id=0, has_side_effects=True, vmem_limit_bytes=60 * 1024 * 1024),
        name="outer_step",
    )(local_weights, base_weights, momentum, scale_codes)
    return pl.pallas_call(
        finish,
        out_shape=(
            jax.ShapeDtypeStruct((ROWS, COLS), jnp.float32),
            jax.ShapeDtypeStruct((ROWS, COLS), jnp.float32),
            jax.ShapeDtypeStruct((FSDP * ROWS, COLS), jnp.bfloat16),
        ),
        in_specs=[vmem] * 3,
        out_specs=(anywhere,) * 3,
        scratch_shapes=[dma((3,))],
        name="write_out",
    )(*results)


def solution(mesh):
    in_specs = (P("rep", "fsdp", None), P("fsdp", None), P("fsdp", None), P("rep", "fsdp", None))
    out_specs = (P("fsdp", None), P("fsdp", None), P())
    return jax.shard_map(step, mesh=mesh, in_specs=in_specs, out_specs=out_specs, check_vma=False)
```

```python
import jax
import jax.numpy as jnp
from jax import lax
from jax.experimental import pallas as pl
from jax.experimental.pallas import tpu as pltpu
from jax.sharding import PartitionSpec as P

outer_rate = 0.7
outer_mu = 0.9
clip_level = 4.0

ROWS = 8
COLS = 6144
LANES = 128
CHIPS = 16
SPAN = COLS // CHIPS
Z = 16
FSDP = 8
REPLICAS = 64
MESH = pl.DeviceIdType.MESH

OFFSETS = sorted(
    [(dx, dy) for dy in range(4) for dx in range(4)],
    key=lambda o: -(min(o[0], 4 - o[0]) + min(o[1], 4 - o[1])),
)


def wait_bytes(ref, sem):
    pltpu.make_async_copy(ref, ref, sem).wait()


def kernel(local_hbm, base_hbm, moment_hbm, codes_hbm, new_base_ref, new_moment_ref, rows,
           local, base, moment, codes, terms0, terms1, arrived0, arrived1, mine0, mine1, parts0, parts1, us,
           load_sem, term_send, term_recv, u_send, u_recv, part_send, part_recv, row_send, row_recv, pass_send, pass_recv):
    rep = lax.axis_index("rep")
    zl = lax.axis_index("fsdp")
    c = rep % 2
    x = (rep // 2) % 4
    zh = (rep // 8) % 2
    y = rep // 16
    z = zh * FSDP + zl
    half = zl // 4
    home = (zl // 2) % 2
    at_home = c == home
    first = (y * 4 + x) * SPAN
    xs = [(x + d) % 4 for d in range(4)]
    ys = [(y + d) % 4 for d in range(4)]

    def in_plane(dx, dy, pc):
        return (ys[dy] * 16 + zh * 8 + xs[dx] * 2 + pc, zl)

    def along_z(d, pc):
        zt = (z + d + Z) % Z
        return (y * 16 + (zt // FSDP) * 8 + x * 2 + pc, zt % FSDP)

    def send(src, dst, send_sem, recv_sem, to):
        pltpu.make_async_remote_copy(
            src_ref=src, dst_ref=dst, send_sem=send_sem, recv_sem=recv_sem, device_id=to, device_id_type=MESH).start()

    loads = [
        pltpu.make_async_copy(src, dst, load_sem.at[i])
        for i, (src, dst) in enumerate(((codes_hbm, codes), (local_hbm, local), (base_hbm, base), (moment_hbm, moment)))
    ]
    for load in loads:
        load.start()

    barrier = pltpu.get_barrier_semaphore()
    for dx, dy in OFFSETS:
        for pc in (c, 1 - c) if (dx, dy) != (0, 0) else (1 - c,):
            pl.semaphore_signal(barrier, inc=1, device_id=in_plane(dx, dy, pc), device_id_type=MESH)
    z_near = (4, -4, 3, -3, 2, -2, 1, -1)
    for d in z_near:
        for pc in (c, 1 - c):
            pl.semaphore_signal(barrier, inc=1, device_id=along_z(d, pc), device_id_type=MESH)

    for load in loads:
        load.wait()

    scales = codes[0].astype(jnp.float32) / 64.0
    inverse = 1.0 / scales

    def term(j):
        cols = slice(j * LANES, (j + 1) * LANES)
        pseudo = base[:, cols] - local[0, :, cols].astype(jnp.float32)
        quantized = jnp.clip(pseudo * inverse[:, j:j + 1], -clip_level, clip_level).astype(jnp.bfloat16)
        return quantized.astype(jnp.float32) * scales[:, j:j + 1]

    for k in range(CHIPS):
        terms0[k] = jnp.concatenate([term(3 * k), term(3 * k + 1)], axis=0).astype(jnp.bfloat16)
        terms1[k] = term(3 * k + 2)

    for j in range(3):
        cols = pl.ds(pl.multiple_of(first + j * LANES, LANES), LANES)
        us[zl, j] = base[:, cols] - (outer_rate * outer_mu * outer_mu) * moment[:, cols]

    pl.semaphore_wait(barrier, 2 * len(z_near) + 2 * CHIPS - 1)

    for dx, dy in OFFSETS:
        k = ys[dy] * 4 + xs[dx]
        slot = (dy * 4 + dx) * 2 - 1
        if (dx, dy) == (0, 0):
            @pl.when(c == 1)
            def _():
                send(terms0.at[k], arrived0.at[0], term_send, term_recv, in_plane(0, 0, 0))

            @pl.when(c == 0)
            def _():
                send(terms1.at[k], arrived1.at[0], term_send, term_recv, in_plane(0, 0, 1))
        else:
            send(terms0.at[k], arrived0.at[slot + c], term_send, term_recv, in_plane(dx, dy, 0))
            send(terms1.at[k], arrived1.at[slot + 1 - c], term_send, term_recv, in_plane(dx, dy, 1))
    for d in (4, 3, -3, 2, -2, 1, -1):
        send(us.at[zl], us.at[zl], u_send, u_recv, along_z(d, c))

    wait_bytes(arrived0, term_recv)
    me = y * 4 + x
    z_far = (8, 7, -7, 6, -6, 5, -5, 4, -4, 3, -3, 2, -2, 1, -1)

    def plane_sum(terms, arrived, mine, parts):
        total = terms[me].astype(jnp.float32)
        for slot in range(2 * CHIPS - 1):
            total += arrived[slot].astype(jnp.float32)
        mine[...] = total.astype(mine.dtype)
        wait_bytes(us.at[0:FSDP - 1], u_recv)

        for d in z_far:
            send(mine, parts.at[z], part_send, part_recv.at[half], along_z(d, home))

        @pl.when(at_home)
        def _():
            parts[z] = mine[...]

        @pl.when(jnp.logical_not(at_home))
        def _():
            send(mine, parts.at[z], part_send, part_recv.at[half], in_plane(0, 0, home))

    @pl.when(c == 0)
    def _():
        plane_sum(terms0, arrived0, mine0, parts0)

    @pl.when(c == 1)
    def _():
        plane_sum(terms1, arrived1, mine1, parts1)

    def sums(f):
        two = parts0[f].astype(jnp.float32) + parts0[f + FSDP].astype(jnp.float32)
        return two[0:ROWS], two[ROWS:2 * ROWS], parts1[f] + parts1[f + FSDP]

    def update(g, slot):
        low, high = sums(2 * g), sums(2 * g + 1)
        factor = outer_rate * (1.0 + outer_mu) / REPLICAS
        for j in range(3):
            cols = pl.ds(pl.multiple_of(first + j * LANES, LANES), LANES)
            pair = jnp.concatenate([us[2 * g, j] - factor * low[j], us[2 * g + 1, j] - factor * high[j]], axis=0)
            rows[slot, :, cols] = pair.astype(jnp.bfloat16)

    mine_cols = pl.ds(pl.multiple_of(first, LANES), SPAN)
    other_cols = slice(0, (CHIPS - 1) * SPAN)

    def spread(block, batch):
        for dx, dy in OFFSETS[:-1]:
            send(block, block, row_send.at[batch], row_recv.at[batch], in_plane(dx, dy, c))

    wait_bytes(arrived0.at[0:8], part_recv.at[1 - half])
    update(2 * (1 - half) + c, c)
    spread(rows.at[c, :, mine_cols], 0)

    @pl.when(at_home)
    def _():
        wait_bytes(arrived0.at[0:7], part_recv.at[half])
        update(2 * half + c, 3)
        for j, total in enumerate(sums(zl)):
            cols = pl.ds(pl.multiple_of(first + j * LANES, LANES), LANES)
            high = total.astype(jnp.bfloat16).astype(jnp.float32)
            rows[4, :, cols] = jnp.concatenate([high, total - high], axis=0).astype(jnp.bfloat16)
        spread(rows.at[3:5, :, mine_cols], 1)

    @pl.when(jnp.logical_not(at_home))
    def _():
        wait_bytes(arrived0.at[0:8], part_recv.at[half])
        update(2 * half + c, 2)
        spread(rows.at[2, :, mine_cols], 1)

    sibling = in_plane(0, 0, 1 - c)
    wait_bytes(rows.at[0, :, other_cols], row_recv.at[0])
    send(rows.at[c], rows.at[c], pass_send.at[0], pass_recv.at[0], sibling)

    @pl.when(at_home)
    def _():
        wait_bytes(rows.at[3:5, :, other_cols], row_recv.at[1])
        send(rows.at[3:5], rows.at[3:5], pass_send.at[1], pass_recv.at[1], sibling)
        wait_bytes(rows.at[2], pass_recv.at[1])

    @pl.when(jnp.logical_not(at_home))
    def _():
        wait_bytes(rows.at[2, :, other_cols], row_recv.at[1])
        send(rows.at[2], rows.at[2], pass_send.at[1], pass_recv.at[1], sibling)
        wait_bytes(rows.at[3:5], pass_recv.at[1])

    wait_bytes(rows.at[0], pass_recv.at[0])

    for j in range(COLS // LANES):
        cols = slice(j * LANES, (j + 1) * LANES)
        split = rows[4, :, cols].astype(jnp.float32)
        average = (split[0:ROWS] + split[ROWS:2 * ROWS]) / REPLICAS
        new_moment = outer_mu * moment[:, cols] + average
        new_moment_ref[:, cols] = new_moment
        new_base_ref[:, cols] = base[:, cols] - outer_rate * (average + outer_mu * new_moment)

    wait_bytes(arrived0, term_send)
    wait_bytes(us.at[0:FSDP - 1], u_send)
    wait_bytes(rows.at[0, :, other_cols], row_send.at[0])
    wait_bytes(rows.at[0], pass_send.at[0])

    @pl.when(at_home)
    def _():
        wait_bytes(arrived0.at[0:15], part_send)
        wait_bytes(rows.at[3:5, :, other_cols], row_send.at[1])
        wait_bytes(rows.at[3:5], pass_send.at[1])

    @pl.when(jnp.logical_not(at_home))
    def _():
        wait_bytes(arrived0.at[0:16], part_send)
        wait_bytes(rows.at[2, :, other_cols], row_send.at[1])
        wait_bytes(rows.at[2], pass_send.at[1])


def finish(new_base, new_moment, rows, new_base_out, new_moment_out, full_out, sems):
    zl = lax.axis_index("fsdp")
    half = zl // 4
    home = (zl // 2) % 2
    groups = (2 - 2 * half, 3 - 2 * half, 2 * half + 1 - home, 2 * half + home)
    copies = [(rows.at[slot], full_out.at[pl.ds(pl.multiple_of(16 * g, 16), 16)]) for slot, g in enumerate(groups)]
    copies += [(new_base, new_base_out), (new_moment, new_moment_out)]
    copies = [pltpu.make_async_copy(src, dst, sems.at[i]) for i, (src, dst) in enumerate(copies)]
    for copy in copies:
        copy.start()
    for copy in copies:
        copy.wait()


def step(local_weights, base_weights, momentum, scale_codes):
    anywhere = pl.BlockSpec(memory_space=pl.ANY)
    vmem = pl.BlockSpec(memory_space=pltpu.VMEM)
    dma = pltpu.SemaphoreType.DMA
    results = pl.pallas_call(
        kernel,
        out_shape=(
            pltpu.VMEM((ROWS, COLS), jnp.float32),
            pltpu.VMEM((ROWS, COLS), jnp.float32),
            pltpu.VMEM((5, 16, COLS), jnp.bfloat16),
        ),
        in_specs=[anywhere] * 4,
        out_specs=(vmem, vmem, vmem),
        scratch_shapes=[
            pltpu.VMEM((1, ROWS, COLS), jnp.bfloat16),
            pltpu.VMEM((ROWS, COLS), jnp.float32),
            pltpu.VMEM((ROWS, COLS), jnp.float32),
            pltpu.VMEM((1, ROWS, COLS // LANES), jnp.int32),
            pltpu.VMEM((CHIPS, 16, LANES), jnp.bfloat16),
            pltpu.VMEM((CHIPS, ROWS, LANES), jnp.float32),
            pltpu.VMEM((2 * CHIPS - 1, 16, LANES), jnp.bfloat16),
            pltpu.VMEM((2 * CHIPS - 1, ROWS, LANES), jnp.float32),
            pltpu.VMEM((16, LANES), jnp.bfloat16),
            pltpu.VMEM((ROWS, LANES), jnp.float32),
            pltpu.VMEM((Z, 16, LANES), jnp.bfloat16),
            pltpu.VMEM((Z, ROWS, LANES), jnp.float32),
            pltpu.VMEM((FSDP, 3, ROWS, LANES), jnp.float32),
            dma((4,)), dma, dma, dma, dma, dma, dma((2,)), dma((2,)), dma((2,)), dma((2,)), dma((2,)),
        ],
        compiler_params=pltpu.CompilerParams(collective_id=0, has_side_effects=True, vmem_limit_bytes=60 * 1024 * 1024),
        name="outer_step",
    )(*(pltpu.with_memory_space_constraint(a, pltpu.HBM) for a in (local_weights, base_weights, momentum, scale_codes)))
    return pl.pallas_call(
        finish,
        out_shape=(
            jax.ShapeDtypeStruct((ROWS, COLS), jnp.float32),
            jax.ShapeDtypeStruct((ROWS, COLS), jnp.float32),
            jax.ShapeDtypeStruct((FSDP * ROWS, COLS), jnp.bfloat16),
        ),
        in_specs=[anywhere] * 3,
        out_specs=(anywhere,) * 3,
        scratch_shapes=[dma((6,))],
        compiler_params=pltpu.CompilerParams(vmem_limit_bytes=1024 * 1024),
        name="write_out",
    )(*(pltpu.with_memory_space_constraint(r, pltpu.VMEM) for r in results))


def solution(mesh):
    in_specs = (P("rep", "fsdp", None), P("fsdp", None), P("fsdp", None), P("rep", "fsdp", None))
    out_specs = (P("fsdp", None), P("fsdp", None), P())
    return jax.shard_map(step, mesh=mesh, in_specs=in_specs, out_specs=out_specs, check_vma=False)
```

```python
import jax
import jax.numpy as jnp
from jax import lax
from jax.experimental import pallas as pl
from jax.experimental.pallas import tpu as pltpu
from jax.sharding import PartitionSpec as P

outer_rate = 0.7
outer_mu = 0.9
clip_level = 4.0

ROWS = 8
COLS = 6144
LANES = 128
CHIPS = 16
SPAN = COLS // CHIPS
Z = 16
FSDP = 8
REPLICAS = 64
MESH = pl.DeviceIdType.MESH

OFFSETS = sorted(
    [(dx, dy) for dy in range(4) for dx in range(4)],
    key=lambda o: -(min(o[0], 4 - o[0]) + min(o[1], 4 - o[1])),
)


def wait_bytes(ref, sem):
    pltpu.make_async_copy(ref, ref, sem).wait()


def kernel(local_hbm, base_hbm, moment_hbm, codes_hbm, new_base_ref, new_moment_ref, rows,
           local, base, moment, codes, terms0, terms1, gotx0, gotx1, column0, column1, goty0, goty1, mine0, mine1,
           parts0, parts1, us, load_sem, greet_sem, x_send, x_recv, y_send, y_recv, u_send, u_recv, part_send, part_recv, row_send, row_recv, pass_send, pass_recv):
    rep = lax.axis_index("rep")
    zl = lax.axis_index("fsdp")
    c = rep % 2
    x = (rep // 2) % 4
    zh = (rep // 8) % 2
    y = rep // 16
    z = zh * FSDP + zl
    half = zl // 4
    home = (zl // 2) % 2
    at_home = c == home
    first = (y * 4 + x) * SPAN
    xs = [(x + d) % 4 for d in range(4)]
    ys = [(y + d) % 4 for d in range(4)]

    def in_plane(dx, dy, pc):
        return (ys[dy] * 16 + zh * 8 + xs[dx] * 2 + pc, zl)

    def along_z(d, pc):
        zt = (z + d + Z) % Z
        return (y * 16 + (zt // FSDP) * 8 + x * 2 + pc, zt % FSDP)

    def send(src, dst, send_sem, recv_sem, to):
        pltpu.make_async_remote_copy(
            src_ref=src, dst_ref=dst, send_sem=send_sem, recv_sem=recv_sem, device_id=to, device_id_type=MESH).start()

    loads = [
        pltpu.make_async_copy(src, dst, load_sem.at[i])
        for i, (src, dst) in enumerate(((codes_hbm, codes), (local_hbm, local), (base_hbm, base), (moment_hbm, moment)))
    ]
    for load in loads:
        load.start()

    barrier = pltpu.get_barrier_semaphore()
    greeted = [along_z(d, pc) for d in (2, -2) for pc in (c, 1 - c)]
    greeted += [in_plane(2, 0, c), in_plane(2, 0, 1 - c), in_plane(0, 2, c)]
    greeted += [along_z(d, pc) for d in (1, -1) for pc in (c, 1 - c)]
    greeted += [in_plane(dx, 0, pc) for dx in (1, 3) for pc in (c, 1 - c)]
    greeted += [in_plane(0, 1, c), in_plane(0, 3, c), in_plane(0, 0, 1 - c)]
    for peer in greeted:
        pl.semaphore_signal(barrier, inc=1, device_id=peer, device_id_type=MESH)

    for load in loads:
        load.wait()

    scales = codes[0].astype(jnp.float32) / 64.0
    inverse = 1.0 / scales

    def term(j):
        cols = slice(j * LANES, (j + 1) * LANES)
        pseudo = base[:, cols] - local[0, :, cols].astype(jnp.float32)
        quantized = jnp.clip(pseudo * inverse[:, j:j + 1], -clip_level, clip_level).astype(jnp.bfloat16)
        return quantized.astype(jnp.float32) * scales[:, j:j + 1]

    for k in range(CHIPS):
        to_y, to_x = k // 4, k % 4
        terms0[to_x, to_y] = jnp.concatenate([term(3 * k), term(3 * k + 1)], axis=0).astype(jnp.bfloat16)
        terms1[to_x, to_y] = term(3 * k + 2)

    for j in range(3):
        cols = pl.ds(pl.multiple_of(first + j * LANES, LANES), LANES)
        us[zl, j] = base[:, cols] - (outer_rate * outer_mu * outer_mu) * moment[:, cols]

    pl.semaphore_wait(barrier, len(greeted))

    for d in (2, -2):
        pl.semaphore_signal(greet_sem.at[0], inc=1, device_id=along_z(d, c), device_id_type=MESH)
    for dx in (2, 1, 3):
        send(terms0.at[xs[dx]], gotx0.at[2 * dx - 1 + c], x_send, x_recv, in_plane(dx, 0, 0))
        send(terms1.at[xs[dx]], gotx1.at[2 * dx - c], x_send, x_recv, in_plane(dx, 0, 1))

    @pl.when(c == 1)
    def _():
        send(terms0.at[x], gotx0.at[0], x_send, x_recv, in_plane(0, 0, 0))

    @pl.when(c == 0)
    def _():
        send(terms1.at[x], gotx1.at[0], x_send, x_recv, in_plane(0, 0, 1))

    pl.semaphore_wait(greet_sem.at[0], 2)
    for d in (4, -4):
        pl.semaphore_signal(greet_sem.at[1], inc=1, device_id=along_z(d, c), device_id_type=MESH)
    for d in (4, 3, -3, 2, -2, 1, -1):
        send(us.at[zl], us.at[zl], u_send, u_recv, along_z(d, c))

    wait_bytes(gotx0, x_recv)
    z_far = (7, -7, 6, -6, 5, -5, 4, -4, 3, -3, 2, -2, 1, -1)

    def plane_sum(terms, gotx, column, goty, mine, parts):
        for dy in (2, 1, 3, 0):
            total = terms[x, ys[dy]].astype(jnp.float32)
            for slot in range(7):
                total += gotx[slot, ys[dy]].astype(jnp.float32)
            if dy:
                column[dy - 1] = total.astype(column.dtype)
                send(column.at[dy - 1], goty.at[dy - 1], y_send, y_recv, in_plane(0, dy, c))
        wait_bytes(goty, y_recv)
        for slot in range(3):
            total += goty[slot].astype(jnp.float32)
        mine[...] = total.astype(mine.dtype)
        pl.semaphore_wait(greet_sem.at[1], 2)

        send(mine, parts.at[z], part_send, part_recv.at[2], along_z(8, 1 - home))
        for i in range(Z - 1):
            zt = i + jnp.where(i >= z, 1, 0)
            to = (y * 16 + (zt // FSDP) * 8 + x * 2 + home, zt % FSDP)
            send(mine, parts.at[z], part_send, part_recv.at[half], to)
        send(mine, parts.at[z], part_send, part_recv.at[jnp.where(at_home, 2, half)], in_plane(0, 0, 1 - c))
        parts[z] = mine[...]

    @pl.when(c == 0)
    def _():
        plane_sum(terms0, gotx0, column0, goty0, mine0, parts0)

    @pl.when(c == 1)
    def _():
        plane_sum(terms1, gotx1, column1, goty1, mine1, parts1)

    def sums(f):
        two = parts0[f].astype(jnp.float32) + parts0[f + FSDP].astype(jnp.float32)
        return two[0:ROWS], two[ROWS:2 * ROWS], parts1[f] + parts1[f + FSDP]

    me = y * 4 + x

    def my_lanes(j):
        return pl.ds(pl.multiple_of(first + j * LANES, LANES), LANES)

    def group(g):
        return pl.ds(pl.multiple_of(16 * g, 16), 16)

    def update(g):
        low, high = sums(2 * g), sums(2 * g + 1)
        factor = outer_rate * (1.0 + outer_mu) / REPLICAS
        for j in range(3):
            pair = jnp.concatenate([us[2 * g, j] - factor * low[j], us[2 * g + 1, j] - factor * high[j]], axis=0)
            rows[group(g), my_lanes(j)] = pair.astype(jnp.bfloat16)

    mine_cols = pl.ds(pl.multiple_of(first, LANES), SPAN)
    other_cols = slice(0, (CHIPS - 1) * SPAN)
    split_rows = slice(64, 80)

    def spread(part, batch):
        block = rows.at[part, mine_cols]
        for i in range(CHIPS - 1):
            k = i + jnp.where(i >= me, 1, 0)
            to = ((k // 4) * 16 + zh * 8 + (k % 4) * 2 + c, zl)
            send(block, block, row_send.at[batch], row_recv.at[batch], to)

    wait_bytes(us.at[0:FSDP - 1], u_recv)
    near, far = 2 * (1 - half) + c, 2 * half + c
    wait_bytes(parts0.at[0:8], part_recv.at[1 - half])
    update(near)
    spread(group(near), 0)

    @pl.when(at_home)
    def _():
        wait_bytes(parts0.at[0:7], part_recv.at[half])
        update(far)
        spread(group(far), 1)

    @pl.when(jnp.logical_not(at_home))
    def _():
        wait_bytes(parts0.at[0:8], part_recv.at[half])
        update(far)
        spread(group(far), 1)
        wait_bytes(parts0.at[0:3], part_recv.at[2])
        for j, total in enumerate(sums(zl)):
            high = total.astype(jnp.bfloat16).astype(jnp.float32)
            rows[split_rows, my_lanes(j)] = jnp.concatenate([high, total - high], axis=0).astype(jnp.bfloat16)
        spread(split_rows, 2)

    any_rows = rows.at[0:16]
    other_rows = rows.at[0:16, other_cols]

    def pass_on(part, batch):
        wait_bytes(other_rows, row_recv.at[batch])
        send(rows.at[part], rows.at[part], pass_send.at[batch], pass_recv.at[batch], in_plane(0, 0, 1 - c))

    pass_on(group(near), 0)
    pass_on(group(far), 1)

    @pl.when(at_home)
    def _():
        wait_bytes(any_rows, pass_recv.at[2])

    @pl.when(jnp.logical_not(at_home))
    def _():
        pass_on(split_rows, 2)

    for j in range(COLS // LANES):
        cols = slice(j * LANES, (j + 1) * LANES)
        split = rows[split_rows, cols].astype(jnp.float32)
        average = (split[0:ROWS] + split[ROWS:2 * ROWS]) / REPLICAS
        new_moment = outer_mu * moment[:, cols] + average
        new_moment_ref[:, cols] = new_moment
        new_base_ref[:, cols] = base[:, cols] - outer_rate * (average + outer_mu * new_moment)

    for batch in range(2):
        wait_bytes(any_rows, pass_recv.at[batch])
    wait_bytes(gotx0, x_send)
    wait_bytes(goty0, y_send)
    wait_bytes(us.at[0:FSDP - 1], u_send)
    wait_bytes(parts0, part_send)
    wait_bytes(parts0.at[0:1], part_send)
    for batch in range(2):
        wait_bytes(other_rows, row_send.at[batch])
        wait_bytes(any_rows, pass_send.at[batch])

    @pl.when(jnp.logical_not(at_home))
    def _():
        wait_bytes(other_rows, row_send.at[2])
        wait_bytes(any_rows, pass_send.at[2])


def finish(new_base, new_moment, rows, new_base_out, new_moment_out, full_out, sems):
    copies = [(rows.at[0:64], full_out), (new_base, new_base_out), (new_moment, new_moment_out)]
    copies = [pltpu.make_async_copy(src, dst, sems.at[i]) for i, (src, dst) in enumerate(copies)]
    for copy in copies:
        copy.start()
    for copy in copies:
        copy.wait()


def step(local_weights, base_weights, momentum, scale_codes):
    anywhere = pl.BlockSpec(memory_space=pl.ANY)
    vmem = pl.BlockSpec(memory_space=pltpu.VMEM)
    dma = pltpu.SemaphoreType.DMA
    results = pl.pallas_call(
        kernel,
        out_shape=(
            pltpu.VMEM((ROWS, COLS), jnp.float32),
            pltpu.VMEM((ROWS, COLS), jnp.float32),
            pltpu.VMEM((80, COLS), jnp.bfloat16),
        ),
        in_specs=[anywhere] * 4,
        out_specs=(vmem, vmem, vmem),
        scratch_shapes=[
            pltpu.VMEM((1, ROWS, COLS), jnp.bfloat16),
            pltpu.VMEM((ROWS, COLS), jnp.float32),
            pltpu.VMEM((ROWS, COLS), jnp.float32),
            pltpu.VMEM((1, ROWS, COLS // LANES), jnp.int32),
            pltpu.VMEM((4, 4, 16, LANES), jnp.bfloat16),
            pltpu.VMEM((4, 4, ROWS, LANES), jnp.float32),
            pltpu.VMEM((7, 4, 16, LANES), jnp.bfloat16),
            pltpu.VMEM((7, 4, ROWS, LANES), jnp.float32),
            pltpu.VMEM((3, 16, LANES), jnp.bfloat16),
            pltpu.VMEM((3, ROWS, LANES), jnp.float32),
            pltpu.VMEM((3, 16, LANES), jnp.bfloat16),
            pltpu.VMEM((3, ROWS, LANES), jnp.float32),
            pltpu.VMEM((16, LANES), jnp.bfloat16),
            pltpu.VMEM((ROWS, LANES), jnp.float32),
            pltpu.VMEM((Z, 16, LANES), jnp.bfloat16),
            pltpu.VMEM((Z, ROWS, LANES), jnp.float32),
            pltpu.VMEM((FSDP, 3, ROWS, LANES), jnp.float32),
            dma((4,)), pltpu.SemaphoreType.REGULAR((2,)), dma, dma, dma, dma, dma, dma, dma, dma((3,)), dma((3,)), dma((3,)), dma((3,)), dma((3,)),
        ],
        compiler_params=pltpu.CompilerParams(collective_id=0, has_side_effects=True, vmem_limit_bytes=60 * 1024 * 1024),
        name="outer_step",
    )(*(pltpu.with_memory_space_constraint(a, pltpu.HBM) for a in (local_weights, base_weights, momentum, scale_codes)))
    return pl.pallas_call(
        finish,
        out_shape=(
            jax.ShapeDtypeStruct((ROWS, COLS), jnp.float32),
            jax.ShapeDtypeStruct((ROWS, COLS), jnp.float32),
            jax.ShapeDtypeStruct((FSDP * ROWS, COLS), jnp.bfloat16),
        ),
        in_specs=[anywhere] * 3,
        out_specs=(anywhere,) * 3,
        scratch_shapes=[dma((3,))],
        compiler_params=pltpu.CompilerParams(vmem_limit_bytes=1024 * 1024),
        name="write_out",
    )(*(pltpu.with_memory_space_constraint(r, pltpu.VMEM) for r in results))


def solution(mesh):
    in_specs = (P("rep", "fsdp", None), P("fsdp", None), P("fsdp", None), P("rep", "fsdp", None))
    out_specs = (P("fsdp", None), P("fsdp", None), P())
    return jax.shard_map(step, mesh=mesh, in_specs=in_specs, out_specs=out_specs, check_vma=False)
```

```python
import jax
import jax.numpy as jnp
from jax import lax
from jax.experimental import pallas as pl
from jax.experimental.pallas import tpu as pltpu
from jax.sharding import PartitionSpec as P

outer_rate = 0.7
outer_mu = 0.9
clip_level = 4.0

ROWS = 8
COLS = 6144
LANES = 128
CHIPS = 16
SPAN = COLS // CHIPS
Z = 16
FSDP = 8
REPLICAS = 64
MESH = pl.DeviceIdType.MESH

OFFSETS = sorted(
    [(dx, dy) for dy in range(4) for dx in range(4)],
    key=lambda o: -(min(o[0], 4 - o[0]) + min(o[1], 4 - o[1])),
)


def wait_bytes(ref, sem):
    pltpu.make_async_copy(ref, ref, sem).wait()


def kernel(local_hbm, base_hbm, moment_hbm, codes_hbm, new_base_ref, new_moment_ref, rows,
           local, base, moment, codes, terms0, terms1, arrived0, arrived1, mine0, mine1,
           parts0, parts1, us, load_sem, greet_sem, x_send, x_recv, u_send, u_recv, part_send, part_recv, row_send, row_recv, pass_send, pass_recv):
    rep = lax.axis_index("rep")
    zl = lax.axis_index("fsdp")
    c = rep % 2
    x = (rep // 2) % 4
    zh = (rep // 8) % 2
    y = rep // 16
    z = zh * FSDP + zl
    half = zl // 4
    home = (zl // 2) % 2
    at_home = c == home
    first = (y * 4 + x) * SPAN
    xs = [(x + d) % 4 for d in range(4)]
    ys = [(y + d) % 4 for d in range(4)]

    def in_plane(dx, dy, pc):
        return (ys[dy] * 16 + zh * 8 + xs[dx] * 2 + pc, zl)

    def along_z(d, pc):
        zt = (z + d + Z) % Z
        return (y * 16 + (zt // FSDP) * 8 + x * 2 + pc, zt % FSDP)

    def send(src, dst, send_sem, recv_sem, to):
        pltpu.make_async_remote_copy(
            src_ref=src, dst_ref=dst, send_sem=send_sem, recv_sem=recv_sem, device_id=to, device_id_type=MESH).start()

    loads = [
        pltpu.make_async_copy(src, dst, load_sem.at[i])
        for i, (src, dst) in enumerate(((codes_hbm, codes), (local_hbm, local), (base_hbm, base), (moment_hbm, moment)))
    ]
    for load in loads:
        load.start()

    barrier = pltpu.get_barrier_semaphore()
    greeted = [in_plane(dx, dy, pc) for dx, dy in OFFSETS[:5] for pc in (c, 1 - c)]
    greeted += [along_z(d, pc) for d in (2, -2) for pc in (c, 1 - c)]
    greeted += [in_plane(dx, dy, pc) for dx, dy in OFFSETS[5:11] for pc in (c, 1 - c)]
    greeted += [along_z(d, pc) for d in (1, -1) for pc in (c, 1 - c)]
    greeted += [in_plane(dx, dy, pc) for dx, dy in OFFSETS[11:15] for pc in (c, 1 - c)]
    greeted += [in_plane(0, 0, 1 - c)]
    for peer in greeted:
        pl.semaphore_signal(barrier, inc=1, device_id=peer, device_id_type=MESH)

    for load in loads:
        load.wait()

    scales = codes[0].astype(jnp.float32) / 64.0
    inverse = 1.0 / scales

    def term(j):
        cols = slice(j * LANES, (j + 1) * LANES)
        pseudo = base[:, cols] - local[0, :, cols].astype(jnp.float32)
        quantized = jnp.clip(pseudo * inverse[:, j:j + 1], -clip_level, clip_level).astype(jnp.bfloat16)
        return quantized.astype(jnp.float32) * scales[:, j:j + 1]

    for k in range(CHIPS):
        terms0[k] = jnp.concatenate([term(3 * k), term(3 * k + 1)], axis=0).astype(jnp.bfloat16)
        terms1[k] = term(3 * k + 2)

    for j in range(3):
        cols = pl.ds(pl.multiple_of(first + j * LANES, LANES), LANES)
        us[zl, j] = base[:, cols] - (outer_rate * outer_mu * outer_mu) * moment[:, cols]

    pl.semaphore_wait(barrier, len(greeted))

    for d in (2, -2):
        pl.semaphore_signal(greet_sem.at[0], inc=1, device_id=along_z(d, c), device_id_type=MESH)

    for dx, dy in OFFSETS[:-1]:
        k = ys[dy] * 4 + xs[dx]
        slot = (dy * 4 + dx) * 2 - 1
        send(terms0.at[k], arrived0.at[slot + c], x_send, x_recv, in_plane(dx, dy, 0))
        send(terms1.at[k], arrived1.at[slot + 1 - c], x_send, x_recv, in_plane(dx, dy, 1))

    me = y * 4 + x

    @pl.when(c == 1)
    def _():
        send(terms0.at[me], arrived0.at[0], x_send, x_recv, in_plane(0, 0, 0))

    @pl.when(c == 0)
    def _():
        send(terms1.at[me], arrived1.at[0], x_send, x_recv, in_plane(0, 0, 1))

    pl.semaphore_wait(greet_sem.at[0], 2)
    for d in (4, -4):
        pl.semaphore_signal(greet_sem.at[1], inc=1, device_id=along_z(d, c), device_id_type=MESH)
    for d in (4, 3, -3, 2, -2, 1, -1):
        send(us.at[zl], us.at[zl], u_send, u_recv, along_z(d, c))

    wait_bytes(arrived0, x_recv)
    z_far = (7, -7, 6, -6, 5, -5, 4, -4, 3, -3, 2, -2, 1, -1)

    def plane_sum(terms, arrived, mine, parts):
        total = terms[me].astype(jnp.float32)
        for slot in range(2 * CHIPS - 1):
            total += arrived[slot].astype(jnp.float32)
        mine[...] = total.astype(mine.dtype)
        pl.semaphore_wait(greet_sem.at[1], 2)

        send(mine, parts.at[z], part_send, part_recv.at[2], along_z(8, 1 - home))
        for i in range(Z - 1):
            zt = i + jnp.where(i >= z, 1, 0)
            to = (y * 16 + (zt // FSDP) * 8 + x * 2 + home, zt % FSDP)
            send(mine, parts.at[z], part_send, part_recv.at[half], to)
        send(mine, parts.at[z], part_send, part_recv.at[jnp.where(at_home, 2, half)], in_plane(0, 0, 1 - c))
        parts[z] = mine[...]

    @pl.when(c == 0)
    def _():
        plane_sum(terms0, arrived0, mine0, parts0)

    @pl.when(c == 1)
    def _():
        plane_sum(terms1, arrived1, mine1, parts1)

    def sums(f):
        two = parts0[f].astype(jnp.float32) + parts0[f + FSDP].astype(jnp.float32)
        return two[0:ROWS], two[ROWS:2 * ROWS], parts1[f] + parts1[f + FSDP]

    def my_lanes(j):
        return pl.ds(pl.multiple_of(first + j * LANES, LANES), LANES)

    def group(g):
        return pl.ds(pl.multiple_of(16 * g, 16), 16)

    def update(g):
        low, high = sums(2 * g), sums(2 * g + 1)
        factor = outer_rate * (1.0 + outer_mu) / REPLICAS
        for j in range(3):
            pair = jnp.concatenate([us[2 * g, j] - factor * low[j], us[2 * g + 1, j] - factor * high[j]], axis=0)
            rows[group(g), my_lanes(j)] = pair.astype(jnp.bfloat16)

    mine_cols = pl.ds(pl.multiple_of(first, LANES), SPAN)
    other_cols = slice(0, (CHIPS - 1) * SPAN)
    split_rows = slice(64, 80)

    def spread(part, batch):
        block = rows.at[part, mine_cols]
        for i in range(CHIPS - 1):
            k = i + jnp.where(i >= me, 1, 0)
            to = ((k // 4) * 16 + zh * 8 + (k % 4) * 2 + c, zl)
            send(block, block, row_send.at[batch], row_recv.at[batch], to)

    wait_bytes(us.at[0:FSDP - 1], u_recv)
    near, far = 2 * (1 - half) + c, 2 * half + c
    wait_bytes(parts0.at[0:8], part_recv.at[1 - half])
    update(near)
    spread(group(near), 0)

    @pl.when(at_home)
    def _():
        wait_bytes(parts0.at[0:7], part_recv.at[half])
        update(far)
        spread(group(far), 1)

    @pl.when(jnp.logical_not(at_home))
    def _():
        wait_bytes(parts0.at[0:8], part_recv.at[half])
        update(far)
        spread(group(far), 1)
        wait_bytes(parts0.at[0:3], part_recv.at[2])
        for j, total in enumerate(sums(zl)):
            high = total.astype(jnp.bfloat16).astype(jnp.float32)
            rows[split_rows, my_lanes(j)] = jnp.concatenate([high, total - high], axis=0).astype(jnp.bfloat16)
        spread(split_rows, 2)

    any_rows = rows.at[0:16]
    other_rows = rows.at[0:16, other_cols]

    def pass_on(part, batch):
        wait_bytes(other_rows, row_recv.at[batch])
        send(rows.at[part], rows.at[part], pass_send.at[batch], pass_recv.at[batch], in_plane(0, 0, 1 - c))

    pass_on(group(near), 0)
    pass_on(group(far), 1)

    @pl.when(at_home)
    def _():
        wait_bytes(any_rows, pass_recv.at[2])

    @pl.when(jnp.logical_not(at_home))
    def _():
        pass_on(split_rows, 2)

    for j in range(COLS // LANES):
        cols = slice(j * LANES, (j + 1) * LANES)
        split = rows[split_rows, cols].astype(jnp.float32)
        average = (split[0:ROWS] + split[ROWS:2 * ROWS]) / REPLICAS
        new_moment = outer_mu * moment[:, cols] + average
        new_moment_ref[:, cols] = new_moment
        new_base_ref[:, cols] = base[:, cols] - outer_rate * (average + outer_mu * new_moment)

    for batch in range(2):
        wait_bytes(any_rows, pass_recv.at[batch])
    wait_bytes(arrived0, x_send)
    wait_bytes(us.at[0:FSDP - 1], u_send)
    wait_bytes(parts0, part_send)
    wait_bytes(parts0.at[0:1], part_send)
    for batch in range(2):
        wait_bytes(other_rows, row_send.at[batch])
        wait_bytes(any_rows, pass_send.at[batch])

    @pl.when(jnp.logical_not(at_home))
    def _():
        wait_bytes(other_rows, row_send.at[2])
        wait_bytes(any_rows, pass_send.at[2])


def finish(new_base, new_moment, rows, new_base_out, new_moment_out, full_out, sems):
    copies = [(rows.at[0:64], full_out), (new_base, new_base_out), (new_moment, new_moment_out)]
    copies = [pltpu.make_async_copy(src, dst, sems.at[i]) for i, (src, dst) in enumerate(copies)]
    for copy in copies:
        copy.start()
    for copy in copies:
        copy.wait()


def step(local_weights, base_weights, momentum, scale_codes):
    anywhere = pl.BlockSpec(memory_space=pl.ANY)
    vmem = pl.BlockSpec(memory_space=pltpu.VMEM)
    dma = pltpu.SemaphoreType.DMA
    results = pl.pallas_call(
        kernel,
        out_shape=(
            pltpu.VMEM((ROWS, COLS), jnp.float32),
            pltpu.VMEM((ROWS, COLS), jnp.float32),
            pltpu.VMEM((80, COLS), jnp.bfloat16),
        ),
        in_specs=[anywhere] * 4,
        out_specs=(vmem, vmem, vmem),
        scratch_shapes=[
            pltpu.VMEM((1, ROWS, COLS), jnp.bfloat16),
            pltpu.VMEM((ROWS, COLS), jnp.float32),
            pltpu.VMEM((ROWS, COLS), jnp.float32),
            pltpu.VMEM((1, ROWS, COLS // LANES), jnp.int32),
            pltpu.VMEM((CHIPS, 16, LANES), jnp.bfloat16),
            pltpu.VMEM((CHIPS, ROWS, LANES), jnp.float32),
            pltpu.VMEM((2 * CHIPS - 1, 16, LANES), jnp.bfloat16),
            pltpu.VMEM((2 * CHIPS - 1, ROWS, LANES), jnp.float32),
            pltpu.VMEM((16, LANES), jnp.bfloat16),
            pltpu.VMEM((ROWS, LANES), jnp.float32),
            pltpu.VMEM((Z, 16, LANES), jnp.bfloat16),
            pltpu.VMEM((Z, ROWS, LANES), jnp.float32),
            pltpu.VMEM((FSDP, 3, ROWS, LANES), jnp.float32),
            dma((4,)), pltpu.SemaphoreType.REGULAR((2,)), dma, dma, dma, dma, dma, dma((3,)), dma((3,)), dma((3,)), dma((3,)), dma((3,)),
        ],
        compiler_params=pltpu.CompilerParams(collective_id=0, has_side_effects=True, vmem_limit_bytes=60 * 1024 * 1024),
        name="outer_step",
    )(*(pltpu.with_memory_space_constraint(a, pltpu.HBM) for a in (local_weights, base_weights, momentum, scale_codes)))
    return pl.pallas_call(
        finish,
        out_shape=(
            jax.ShapeDtypeStruct((ROWS, COLS), jnp.float32),
            jax.ShapeDtypeStruct((ROWS, COLS), jnp.float32),
            jax.ShapeDtypeStruct((FSDP * ROWS, COLS), jnp.bfloat16),
        ),
        in_specs=[anywhere] * 3,
        out_specs=(anywhere,) * 3,
        scratch_shapes=[dma((3,))],
        compiler_params=pltpu.CompilerParams(vmem_limit_bytes=1024 * 1024),
        name="write_out",
    )(*(pltpu.with_memory_space_constraint(r, pltpu.VMEM) for r in results))


def solution(mesh):
    in_specs = (P("rep", "fsdp", None), P("fsdp", None), P("fsdp", None), P("rep", "fsdp", None))
    out_specs = (P("fsdp", None), P("fsdp", None), P())
    return jax.shard_map(step, mesh=mesh, in_specs=in_specs, out_specs=out_specs, check_vma=False)
```

```python
import jax
import jax.numpy as jnp
from jax import lax
from jax.experimental import pallas as pl
from jax.experimental.pallas import tpu as pltpu
from jax.sharding import PartitionSpec as P

outer_rate = 0.7
outer_mu = 0.9
clip_level = 4.0

ROWS = 8
COLS = 6144
LANES = 128
CHIPS = 16
SPAN = COLS // CHIPS
Z = 16
FSDP = 8
REPLICAS = 64
MESH = pl.DeviceIdType.MESH
FIRST = 11

OFFSETS = sorted(
    [(dx, dy) for dy in range(4) for dx in range(4)],
    key=lambda o: -(min(o[0], 4 - o[0]) + min(o[1], 4 - o[1])),
)


def wait_bytes(ref, sem):
    pltpu.make_async_copy(ref, ref, sem).wait()


def kernel(local_hbm, base_hbm, moment_hbm, codes_hbm, new_base_ref, new_moment_ref, rows,
           local, base, moment, codes, terms0, terms1, arrived0, arrived1, mine0, mine1,
           parts0, parts1, us, load_sem, greet_sem, x_send, x_recv, u_send, u_recv, part_send, part_recv, row_send, row_recv, pass_send, pass_recv):
    rep = lax.axis_index("rep")
    zl = lax.axis_index("fsdp")
    c = rep % 2
    x = (rep // 2) % 4
    zh = (rep // 8) % 2
    y = rep // 16
    z = zh * FSDP + zl
    half = zl // 4
    home = (zl // 2) % 2
    at_home = c == home
    first = (y * 4 + x) * SPAN
    xs = [(x + d) % 4 for d in range(4)]
    ys = [(y + d) % 4 for d in range(4)]

    def in_plane(dx, dy, pc):
        return (ys[dy] * 16 + zh * 8 + xs[dx] * 2 + pc, zl)

    def along_z(d, pc):
        zt = (z + d + Z) % Z
        return (y * 16 + (zt // FSDP) * 8 + x * 2 + pc, zt % FSDP)

    def send(src, dst, send_sem, recv_sem, to):
        pltpu.make_async_remote_copy(
            src_ref=src, dst_ref=dst, send_sem=send_sem, recv_sem=recv_sem, device_id=to, device_id_type=MESH).start()

    loads = [
        pltpu.make_async_copy(src, dst, load_sem.at[i])
        for i, (src, dst) in enumerate(((codes_hbm, codes), (local_hbm, local), (base_hbm, base), (moment_hbm, moment)))
    ]
    for load in loads:
        load.start()

    barrier = pltpu.get_barrier_semaphore()
    greeted = [in_plane(dx, dy, c) for dx, dy in OFFSETS[:5]]
    greeted += [along_z(2, c), along_z(-2, c)]
    greeted += [in_plane(dx, dy, c) for dx, dy in OFFSETS[5:15]]
    greeted += [along_z(1, c), along_z(-1, c), in_plane(0, 0, 1 - c)]
    for peer in greeted:
        pl.semaphore_signal(barrier, inc=1, device_id=peer, device_id_type=MESH)

    for load in loads:
        load.wait()

    scales = codes[0].astype(jnp.float32) / 64.0
    inverse = 1.0 / scales

    def term(j):
        cols = slice(j * LANES, (j + 1) * LANES)
        pseudo = base[:, cols] - local[0, :, cols].astype(jnp.float32)
        quantized = jnp.clip(pseudo * inverse[:, j:j + 1], -clip_level, clip_level).astype(jnp.bfloat16)
        return quantized.astype(jnp.float32) * scales[:, j:j + 1]

    for k in range(CHIPS):
        terms0[k] = jnp.concatenate([term(3 * k), term(3 * k + 1)], axis=0).astype(jnp.bfloat16)
        terms1[k] = term(3 * k + 2)

    for j in range(3):
        cols = pl.ds(pl.multiple_of(first + j * LANES, LANES), LANES)
        us[zl, j] = base[:, cols] - (outer_rate * outer_mu * outer_mu) * moment[:, cols]

    pl.semaphore_wait(barrier, len(greeted))

    pl.semaphore_signal(greet_sem.at[2], inc=1, device_id=in_plane(0, 0, 1 - c), device_id_type=MESH)

    def to_core(offsets, pc):
        @pl.when(pc == 0)
        def _():
            for dx, dy in offsets:
                slot = (dy * 4 + dx) * 2 - 1
                send(terms0.at[ys[dy] * 4 + xs[dx]], arrived0.at[slot + c], x_send, x_recv, in_plane(dx, dy, 0))

        @pl.when(pc == 1)
        def _():
            for dx, dy in offsets:
                slot = (dy * 4 + dx) * 2 - 1
                send(terms1.at[ys[dy] * 4 + xs[dx]], arrived1.at[slot + 1 - c], x_send, x_recv, in_plane(dx, dy, 1))

    to_core(OFFSETS[:FIRST], c)
    pl.semaphore_wait(greet_sem.at[2], 1)
    for d in (2, -2):
        pl.semaphore_signal(greet_sem.at[0], inc=1, device_id=along_z(d, c), device_id_type=MESH)
    to_core(OFFSETS[:FIRST], 1 - c)
    to_core(OFFSETS[FIRST:-1], c)
    to_core(OFFSETS[FIRST:-1], 1 - c)

    me = y * 4 + x

    @pl.when(c == 1)
    def _():
        send(terms0.at[me], arrived0.at[0], x_send, x_recv, in_plane(0, 0, 0))

    @pl.when(c == 0)
    def _():
        send(terms1.at[me], arrived1.at[0], x_send, x_recv, in_plane(0, 0, 1))

    pl.semaphore_wait(greet_sem.at[0], 2)
    for d in (4, -4):
        pl.semaphore_signal(greet_sem.at[1], inc=1, device_id=along_z(d, c), device_id_type=MESH)
    for d in (4, 3, -3, 2, -2, 1, -1):
        send(us.at[zl], us.at[zl], u_send, u_recv, along_z(d, c))

    wait_bytes(arrived0, x_recv)
    z_far = (7, -7, 6, -6, 5, -5, 4, -4, 3, -3, 2, -2, 1, -1)

    def plane_sum(terms, arrived, mine, parts):
        total = terms[me].astype(jnp.float32)
        for slot in range(2 * CHIPS - 1):
            total += arrived[slot].astype(jnp.float32)
        mine[...] = total.astype(mine.dtype)
        pl.semaphore_wait(greet_sem.at[1], 2)

        send(mine, parts.at[z], part_send, part_recv.at[2], along_z(8, 1 - home))
        for i in range(Z - 1):
            zt = i + jnp.where(i >= z, 1, 0)
            to = (y * 16 + (zt // FSDP) * 8 + x * 2 + home, zt % FSDP)
            send(mine, parts.at[z], part_send, part_recv.at[half], to)
        send(mine, parts.at[z], part_send, part_recv.at[jnp.where(at_home, 2, half)], in_plane(0, 0, 1 - c))
        parts[z] = mine[...]

    @pl.when(c == 0)
    def _():
        plane_sum(terms0, arrived0, mine0, parts0)

    @pl.when(c == 1)
    def _():
        plane_sum(terms1, arrived1, mine1, parts1)

    def sums(f):
        two = parts0[f].astype(jnp.float32) + parts0[f + FSDP].astype(jnp.float32)
        return two[0:ROWS], two[ROWS:2 * ROWS], parts1[f] + parts1[f + FSDP]

    def my_lanes(j):
        return pl.ds(pl.multiple_of(first + j * LANES, LANES), LANES)

    def group(g):
        return pl.ds(pl.multiple_of(16 * g, 16), 16)

    def update(g):
        low, high = sums(2 * g), sums(2 * g + 1)
        factor = outer_rate * (1.0 + outer_mu) / REPLICAS
        for j in range(3):
            pair = jnp.concatenate([us[2 * g, j] - factor * low[j], us[2 * g + 1, j] - factor * high[j]], axis=0)
            rows[group(g), my_lanes(j)] = pair.astype(jnp.bfloat16)

    mine_cols = pl.ds(pl.multiple_of(first, LANES), SPAN)
    other_cols = slice(0, (CHIPS - 1) * SPAN)
    split_rows = slice(64, 80)

    def spread(part, batch):
        block = rows.at[part, mine_cols]
        for i in range(CHIPS - 1):
            k = i + jnp.where(i >= me, 1, 0)
            to = ((k // 4) * 16 + zh * 8 + (k % 4) * 2 + c, zl)
            send(block, block, row_send.at[batch], row_recv.at[batch], to)

    wait_bytes(us.at[0:FSDP - 1], u_recv)
    near, far = 2 * (1 - half) + c, 2 * half + c
    wait_bytes(parts0.at[0:8], part_recv.at[1 - half])
    update(near)
    spread(group(near), 0)

    @pl.when(at_home)
    def _():
        wait_bytes(parts0.at[0:7], part_recv.at[half])
        update(far)
        spread(group(far), 1)

    @pl.when(jnp.logical_not(at_home))
    def _():
        wait_bytes(parts0.at[0:8], part_recv.at[half])
        update(far)
        spread(group(far), 1)
        wait_bytes(parts0.at[0:3], part_recv.at[2])
        for j, total in enumerate(sums(zl)):
            high = total.astype(jnp.bfloat16).astype(jnp.float32)
            rows[split_rows, my_lanes(j)] = jnp.concatenate([high, total - high], axis=0).astype(jnp.bfloat16)
        spread(split_rows, 2)

    any_rows = rows.at[0:16]
    other_rows = rows.at[0:16, other_cols]

    def pass_on(part, batch):
        wait_bytes(other_rows, row_recv.at[batch])
        send(rows.at[part], rows.at[part], pass_send.at[batch], pass_recv.at[batch], in_plane(0, 0, 1 - c))

    pass_on(group(near), 0)
    pass_on(group(far), 1)

    @pl.when(at_home)
    def _():
        wait_bytes(any_rows, pass_recv.at[2])

    @pl.when(jnp.logical_not(at_home))
    def _():
        pass_on(split_rows, 2)

    for j in range(COLS // LANES):
        cols = slice(j * LANES, (j + 1) * LANES)
        split = rows[split_rows, cols].astype(jnp.float32)
        average = (split[0:ROWS] + split[ROWS:2 * ROWS]) / REPLICAS
        new_moment = outer_mu * moment[:, cols] + average
        new_moment_ref[:, cols] = new_moment
        new_base_ref[:, cols] = base[:, cols] - outer_rate * (average + outer_mu * new_moment)

    for batch in range(2):
        wait_bytes(any_rows, pass_recv.at[batch])
    wait_bytes(arrived0, x_send)
    wait_bytes(us.at[0:FSDP - 1], u_send)
    wait_bytes(parts0, part_send)
    wait_bytes(parts0.at[0:1], part_send)
    for batch in range(2):
        wait_bytes(other_rows, row_send.at[batch])
        wait_bytes(any_rows, pass_send.at[batch])

    @pl.when(jnp.logical_not(at_home))
    def _():
        wait_bytes(other_rows, row_send.at[2])
        wait_bytes(any_rows, pass_send.at[2])


def finish(new_base, new_moment, rows, new_base_out, new_moment_out, full_out, sems):
    copies = [(rows.at[0:64], full_out), (new_base, new_base_out), (new_moment, new_moment_out)]
    copies = [pltpu.make_async_copy(src, dst, sems.at[i]) for i, (src, dst) in enumerate(copies)]
    for copy in copies:
        copy.start()
    for copy in copies:
        copy.wait()


def step(local_weights, base_weights, momentum, scale_codes):
    anywhere = pl.BlockSpec(memory_space=pl.ANY)
    vmem = pl.BlockSpec(memory_space=pltpu.VMEM)
    dma = pltpu.SemaphoreType.DMA
    results = pl.pallas_call(
        kernel,
        out_shape=(
            pltpu.VMEM((ROWS, COLS), jnp.float32),
            pltpu.VMEM((ROWS, COLS), jnp.float32),
            pltpu.VMEM((80, COLS), jnp.bfloat16),
        ),
        in_specs=[anywhere] * 4,
        out_specs=(vmem, vmem, vmem),
        scratch_shapes=[
            pltpu.VMEM((1, ROWS, COLS), jnp.bfloat16),
            pltpu.VMEM((ROWS, COLS), jnp.float32),
            pltpu.VMEM((ROWS, COLS), jnp.float32),
            pltpu.VMEM((1, ROWS, COLS // LANES), jnp.int32),
            pltpu.VMEM((CHIPS, 16, LANES), jnp.bfloat16),
            pltpu.VMEM((CHIPS, ROWS, LANES), jnp.float32),
            pltpu.VMEM((2 * CHIPS - 1, 16, LANES), jnp.bfloat16),
            pltpu.VMEM((2 * CHIPS - 1, ROWS, LANES), jnp.float32),
            pltpu.VMEM((16, LANES), jnp.bfloat16),
            pltpu.VMEM((ROWS, LANES), jnp.float32),
            pltpu.VMEM((Z, 16, LANES), jnp.bfloat16),
            pltpu.VMEM((Z, ROWS, LANES), jnp.float32),
            pltpu.VMEM((FSDP, 3, ROWS, LANES), jnp.float32),
            dma((4,)), pltpu.SemaphoreType.REGULAR((3,)), dma, dma, dma, dma, dma, dma((3,)), dma((3,)), dma((3,)), dma((3,)), dma((3,)),
        ],
        compiler_params=pltpu.CompilerParams(collective_id=0, has_side_effects=True, vmem_limit_bytes=60 * 1024 * 1024),
        name="outer_step",
    )(*(pltpu.with_memory_space_constraint(a, pltpu.HBM) for a in (local_weights, base_weights, momentum, scale_codes)))
    return pl.pallas_call(
        finish,
        out_shape=(
            jax.ShapeDtypeStruct((ROWS, COLS), jnp.float32),
            jax.ShapeDtypeStruct((ROWS, COLS), jnp.float32),
            jax.ShapeDtypeStruct((FSDP * ROWS, COLS), jnp.bfloat16),
        ),
        in_specs=[anywhere] * 3,
        out_specs=(anywhere,) * 3,
        scratch_shapes=[dma((3,))],
        compiler_params=pltpu.CompilerParams(vmem_limit_bytes=1024 * 1024),
        name="write_out",
    )(*(pltpu.with_memory_space_constraint(r, pltpu.VMEM) for r in results))


def solution(mesh):
    in_specs = (P("rep", "fsdp", None), P("fsdp", None), P("fsdp", None), P("rep", "fsdp", None))
    out_specs = (P("fsdp", None), P("fsdp", None), P())
    return jax.shard_map(step, mesh=mesh, in_specs=in_specs, out_specs=out_specs, check_vma=False)
```

```python
import jax
import jax.numpy as jnp
from jax import lax
from jax.experimental import pallas as pl
from jax.experimental.pallas import tpu as pltpu
from jax.sharding import PartitionSpec as P

outer_rate = 0.7
outer_mu = 0.9
clip_level = 4.0

ROWS = 8
COLS = 6144
LANES = 128
CHIPS = 16
SPAN = COLS // CHIPS
Z = 16
FSDP = 8
REPLICAS = 64
MESH = pl.DeviceIdType.MESH
FIRST = 11

OFFSETS = sorted(
    [(dx, dy) for dy in range(4) for dx in range(4)],
    key=lambda o: -(min(o[0], 4 - o[0]) + min(o[1], 4 - o[1])),
)


def wait_bytes(ref, sem):
    pltpu.make_async_copy(ref, ref, sem).wait()


def kernel(local_hbm, base_hbm, moment_hbm, codes_hbm, new_base_ref, new_moment_ref, rows,
           local, base, moment, codes, terms0, terms1, arrived0, arrived1, mine0, mine1,
           parts0, parts1, us, load_sem, greet_sem, x_send, x_recv, u_send, u_recv, part_send, part_recv, row_send, row_recv, pass_send, pass_recv):
    rep = lax.axis_index("rep")
    zl = lax.axis_index("fsdp")
    c = rep % 2
    x = (rep // 2) % 4
    zh = (rep // 8) % 2
    y = rep // 16
    z = zh * FSDP + zl
    half = zl // 4
    home = (zl // 2) % 2
    at_home = c == home
    first = (y * 4 + x) * SPAN
    xs = [(x + d) % 4 for d in range(4)]
    ys = [(y + d) % 4 for d in range(4)]

    def in_plane(dx, dy, pc):
        return (ys[dy] * 16 + zh * 8 + xs[dx] * 2 + pc, zl)

    def along_z(d, pc):
        zt = (z + d + Z) % Z
        return (y * 16 + (zt // FSDP) * 8 + x * 2 + pc, zt % FSDP)

    def send(src, dst, send_sem, recv_sem, to):
        pltpu.make_async_remote_copy(
            src_ref=src, dst_ref=dst, send_sem=send_sem, recv_sem=recv_sem, device_id=to, device_id_type=MESH).start()

    loads = [
        pltpu.make_async_copy(src, dst, load_sem.at[i])
        for i, (src, dst) in enumerate(((codes_hbm, codes), (local_hbm, local), (base_hbm, base), (moment_hbm, moment)))
    ]
    barrier = pltpu.get_barrier_semaphore()
    greeted = [in_plane(dx, dy, c) for dx, dy in OFFSETS[:5]]
    greeted += [along_z(2, c), along_z(-2, c)]
    greeted += [in_plane(dx, dy, c) for dx, dy in OFFSETS[5:15]]
    greeted += [along_z(1, c), along_z(-1, c), in_plane(0, 0, 1 - c)]
    for i, peer in enumerate(greeted):
        pl.semaphore_signal(barrier, inc=1, device_id=peer, device_id_type=MESH)
        if i == 6:
            for load in loads:
                load.start()

    for load in loads:
        load.wait()

    scales = codes[0].astype(jnp.float32) / 64.0
    inverse = 1.0 / scales

    def term(j):
        cols = slice(j * LANES, (j + 1) * LANES)
        pseudo = base[:, cols] - local[0, :, cols].astype(jnp.float32)
        quantized = jnp.clip(pseudo * inverse[:, j:j + 1], -clip_level, clip_level).astype(jnp.bfloat16)
        return quantized.astype(jnp.float32) * scales[:, j:j + 1]

    for k in range(CHIPS):
        terms0[k] = jnp.concatenate([term(3 * k), term(3 * k + 1)], axis=0).astype(jnp.bfloat16)
        terms1[k] = term(3 * k + 2)

    for j in range(3):
        cols = pl.ds(pl.multiple_of(first + j * LANES, LANES), LANES)
        us[zl, j] = base[:, cols] - (outer_rate * outer_mu * outer_mu) * moment[:, cols]

    pl.semaphore_wait(barrier, len(greeted))

    pl.semaphore_signal(greet_sem.at[2], inc=1, device_id=in_plane(0, 0, 1 - c), device_id_type=MESH)

    def to_core(offsets, pc):
        @pl.when(pc == 0)
        def _():
            for dx, dy in offsets:
                slot = (dy * 4 + dx) * 2 - 1
                send(terms0.at[ys[dy] * 4 + xs[dx]], arrived0.at[slot + c], x_send, x_recv, in_plane(dx, dy, 0))

        @pl.when(pc == 1)
        def _():
            for dx, dy in offsets:
                slot = (dy * 4 + dx) * 2 - 1
                send(terms1.at[ys[dy] * 4 + xs[dx]], arrived1.at[slot + 1 - c], x_send, x_recv, in_plane(dx, dy, 1))

    to_core(OFFSETS[:FIRST], c)
    pl.semaphore_wait(greet_sem.at[2], 1)
    for d in (2, -2):
        pl.semaphore_signal(greet_sem.at[0], inc=1, device_id=along_z(d, c), device_id_type=MESH)
    to_core(OFFSETS[:FIRST], 1 - c)
    to_core(OFFSETS[FIRST:-1], c)
    to_core(OFFSETS[FIRST:-1], 1 - c)

    me = y * 4 + x

    @pl.when(c == 1)
    def _():
        send(terms0.at[me], arrived0.at[0], x_send, x_recv, in_plane(0, 0, 0))

    @pl.when(c == 0)
    def _():
        send(terms1.at[me], arrived1.at[0], x_send, x_recv, in_plane(0, 0, 1))

    pl.semaphore_wait(greet_sem.at[0], 2)
    for d in (4, -4):
        pl.semaphore_signal(greet_sem.at[1], inc=1, device_id=along_z(d, c), device_id_type=MESH)
    for d in (4, 3, -3, 2, -2, 1, -1):
        send(us.at[zl], us.at[zl], u_send, u_recv, along_z(d, c))

    wait_bytes(arrived0, x_recv)
    z_far = (7, -7, 6, -6, 5, -5, 4, -4, 3, -3, 2, -2, 1, -1)

    def plane_sum(terms, arrived, mine, parts):
        total = terms[me].astype(jnp.float32)
        for slot in range(2 * CHIPS - 1):
            total += arrived[slot].astype(jnp.float32)
        mine[...] = total.astype(mine.dtype)
        pl.semaphore_wait(greet_sem.at[1], 2)

        send(mine, parts.at[z], part_send, part_recv.at[2], along_z(8, 1 - home))
        for i in range(Z - 1):
            zt = i + jnp.where(i >= z, 1, 0)
            to = (y * 16 + (zt // FSDP) * 8 + x * 2 + home, zt % FSDP)
            send(mine, parts.at[z], part_send, part_recv.at[half], to)
        send(mine, parts.at[z], part_send, part_recv.at[jnp.where(at_home, 2, half)], in_plane(0, 0, 1 - c))
        parts[z] = mine[...]

    @pl.when(c == 0)
    def _():
        plane_sum(terms0, arrived0, mine0, parts0)

    @pl.when(c == 1)
    def _():
        plane_sum(terms1, arrived1, mine1, parts1)

    def sums(f):
        two = parts0[f].astype(jnp.float32) + parts0[f + FSDP].astype(jnp.float32)
        return two[0:ROWS], two[ROWS:2 * ROWS], parts1[f] + parts1[f + FSDP]

    def my_lanes(j):
        return pl.ds(pl.multiple_of(first + j * LANES, LANES), LANES)

    def group(g):
        return pl.ds(pl.multiple_of(16 * g, 16), 16)

    def update(g):
        low, high = sums(2 * g), sums(2 * g + 1)
        factor = outer_rate * (1.0 + outer_mu) / REPLICAS
        for j in range(3):
            pair = jnp.concatenate([us[2 * g, j] - factor * low[j], us[2 * g + 1, j] - factor * high[j]], axis=0)
            rows[group(g), my_lanes(j)] = pair.astype(jnp.bfloat16)

    mine_cols = pl.ds(pl.multiple_of(first, LANES), SPAN)
    other_cols = slice(0, (CHIPS - 1) * SPAN)
    split_rows = slice(64, 80)

    def spread(part, batch):
        block = rows.at[part, mine_cols]
        for i in range(CHIPS - 1):
            k = i + jnp.where(i >= me, 1, 0)
            to = ((k // 4) * 16 + zh * 8 + (k % 4) * 2 + c, zl)
            send(block, block, row_send.at[batch], row_recv.at[2 * batch + me // 8], to)

    wait_bytes(us.at[0:FSDP - 1], u_recv)
    near, far = 2 * (1 - half) + c, 2 * half + c
    wait_bytes(parts0.at[0:8], part_recv.at[1 - half])
    update(near)
    spread(group(near), 0)

    @pl.when(at_home)
    def _():
        wait_bytes(parts0.at[0:7], part_recv.at[half])
        update(far)
        spread(group(far), 1)

    @pl.when(jnp.logical_not(at_home))
    def _():
        wait_bytes(parts0.at[0:8], part_recv.at[half])
        update(far)
        spread(group(far), 1)
        wait_bytes(parts0.at[0:3], part_recv.at[2])
        for j, total in enumerate(sums(zl)):
            high = total.astype(jnp.bfloat16).astype(jnp.float32)
            rows[split_rows, my_lanes(j)] = jnp.concatenate([high, total - high], axis=0).astype(jnp.bfloat16)
        spread(split_rows, 2)

    any_rows = rows.at[0:16]
    other_rows = rows.at[0:16, other_cols]

    def pass_on(part, batch):
        for upper in range(2):
            arrival = row_recv.at[2 * batch + upper]

            @pl.when(me // 8 == upper)
            def _():
                wait_bytes(rows.at[0:16, 0:7 * SPAN], arrival)

            @pl.when(me // 8 != upper)
            def _():
                wait_bytes(rows.at[0:16, 0:8 * SPAN], arrival)

            block = rows.at[part, upper * 8 * SPAN:(upper + 1) * 8 * SPAN]
            send(block, block, pass_send.at[batch], pass_recv.at[batch], in_plane(0, 0, 1 - c))

    pass_on(group(near), 0)
    pass_on(group(far), 1)

    @pl.when(at_home)
    def _():
        wait_bytes(any_rows, pass_recv.at[2])

    @pl.when(jnp.logical_not(at_home))
    def _():
        pass_on(split_rows, 2)

    for j in range(COLS // LANES):
        cols = slice(j * LANES, (j + 1) * LANES)
        split = rows[split_rows, cols].astype(jnp.float32)
        average = (split[0:ROWS] + split[ROWS:2 * ROWS]) / REPLICAS
        new_moment = outer_mu * moment[:, cols] + average
        new_moment_ref[:, cols] = new_moment
        new_base_ref[:, cols] = base[:, cols] - outer_rate * (average + outer_mu * new_moment)

    for batch in range(2):
        wait_bytes(any_rows, pass_recv.at[batch])
    wait_bytes(arrived0, x_send)
    wait_bytes(us.at[0:FSDP - 1], u_send)
    wait_bytes(parts0, part_send)
    wait_bytes(parts0.at[0:1], part_send)
    for batch in range(2):
        wait_bytes(other_rows, row_send.at[batch])
        wait_bytes(any_rows, pass_send.at[batch])

    @pl.when(jnp.logical_not(at_home))
    def _():
        wait_bytes(other_rows, row_send.at[2])
        wait_bytes(any_rows, pass_send.at[2])


def finish(new_base, new_moment, rows, new_base_out, new_moment_out, full_out, sems):
    copies = [(rows.at[0:64], full_out), (new_base, new_base_out), (new_moment, new_moment_out)]
    copies = [pltpu.make_async_copy(src, dst, sems.at[i]) for i, (src, dst) in enumerate(copies)]
    for copy in copies:
        copy.start()
    for copy in copies:
        copy.wait()


def step(local_weights, base_weights, momentum, scale_codes):
    anywhere = pl.BlockSpec(memory_space=pl.ANY)
    vmem = pl.BlockSpec(memory_space=pltpu.VMEM)
    dma = pltpu.SemaphoreType.DMA
    results = pl.pallas_call(
        kernel,
        out_shape=(
            pltpu.VMEM((ROWS, COLS), jnp.float32),
            pltpu.VMEM((ROWS, COLS), jnp.float32),
            pltpu.VMEM((80, COLS), jnp.bfloat16),
        ),
        in_specs=[anywhere] * 4,
        out_specs=(vmem, vmem, vmem),
        scratch_shapes=[
            pltpu.VMEM((1, ROWS, COLS), jnp.bfloat16),
            pltpu.VMEM((ROWS, COLS), jnp.float32),
            pltpu.VMEM((ROWS, COLS), jnp.float32),
            pltpu.VMEM((1, ROWS, COLS // LANES), jnp.int32),
            pltpu.VMEM((CHIPS, 16, LANES), jnp.bfloat16),
            pltpu.VMEM((CHIPS, ROWS, LANES), jnp.float32),
            pltpu.VMEM((2 * CHIPS - 1, 16, LANES), jnp.bfloat16),
            pltpu.VMEM((2 * CHIPS - 1, ROWS, LANES), jnp.float32),
            pltpu.VMEM((16, LANES), jnp.bfloat16),
            pltpu.VMEM((ROWS, LANES), jnp.float32),
            pltpu.VMEM((Z, 16, LANES), jnp.bfloat16),
            pltpu.VMEM((Z, ROWS, LANES), jnp.float32),
            pltpu.VMEM((FSDP, 3, ROWS, LANES), jnp.float32),
            dma((4,)), pltpu.SemaphoreType.REGULAR((3,)), dma, dma, dma, dma, dma, dma((3,)), dma((3,)), dma((6,)), dma((3,)), dma((3,)),
        ],
        compiler_params=pltpu.CompilerParams(collective_id=0, has_side_effects=True, vmem_limit_bytes=60 * 1024 * 1024),
        name="outer_step",
    )(*(pltpu.with_memory_space_constraint(a, pltpu.HBM) for a in (local_weights, base_weights, momentum, scale_codes)))
    return pl.pallas_call(
        finish,
        out_shape=(
            jax.ShapeDtypeStruct((ROWS, COLS), jnp.float32),
            jax.ShapeDtypeStruct((ROWS, COLS), jnp.float32),
            jax.ShapeDtypeStruct((FSDP * ROWS, COLS), jnp.bfloat16),
        ),
        in_specs=[anywhere] * 3,
        out_specs=(anywhere,) * 3,
        scratch_shapes=[dma((3,))],
        compiler_params=pltpu.CompilerParams(vmem_limit_bytes=1024 * 1024),
        name="write_out",
    )(*(pltpu.with_memory_space_constraint(r, pltpu.VMEM) for r in results))


def solution(mesh):
    in_specs = (P("rep", "fsdp", None), P("fsdp", None), P("fsdp", None), P("rep", "fsdp", None))
    out_specs = (P("fsdp", None), P("fsdp", None), P())
    return jax.shard_map(step, mesh=mesh, in_specs=in_specs, out_specs=out_specs, check_vma=False)
```
